128 devices in a mesh: dp: 16 (over z, y), opt: 8 (over x, core).
Axes of the slice: x: 4, y: 4, z: 4, core: 2. Of those that a mesh axis runs over, the one named last changes fastest.
Arguments:
- grad_partial: bfloat16 [16, 96, 512, 512], P('dp', None, 'opt'), may hold values from -9 to 9
- master: float32 [96, 512, 512], P('dp', 'opt'), may hold values from -6 to 6
- second_moment: float32 [96, 512, 512], P('dp', 'opt'), may hold values from 0.01 to 1000
- owner_table: int32 [96, 1], replicated, may hold values from 0 to 7; in each aligned block of 6 rows (0 to 5, 6 to 11, ...) at most 2 rows name the same one
- factor_left: float32 [16, 8, 2, 512, 512], P('dp', 'opt'), may hold values from -0.2 to 2, as said below
- factor_right: float32 [16, 8, 2, 512, 512], P('dp', 'opt'), may hold values from -0.2 to 2, as said below
- root_left: bfloat16 [16, 8, 2, 512, 512], P('dp', 'opt'), may hold values from -0.15 to 1.5, as said below
- root_right: bfloat16 [16, 8, 2, 512, 512], P('dp', 'opt'), may hold values from -0.15 to 1.5, as said below
Outputs:
- master_new: float32 [96, 512, 512], P('dp', 'opt')
- moment_new: float32 [96, 512, 512], P('dp', 'opt')
- weights: bfloat16 [96, 512, 512], P(None, 'opt')
- left_new: float32 [16, 8, 2, 512, 512], P('dp', 'opt')
- right_new: float32 [16, 8, 2, 512, 512], P('dp', 'opt')
The draws below stay inside these ranges and needn't reach their ends.
Inputs may be any that keep to these rules, and one draw needn't show every extreme that they name: `owner_table`: among the 6 blocks b = i * 6 to i * 6 + 5 of each i, no owner appears more than 2 times, and in every draw some owner appears exactly 2 times. `factor_left`: symmetric in the last two dimensions. `factor_right`: symmetric in the last two dimensions. `root_left`: symmetric in the last two dimensions. `root_right`: symmetric in the last two dimensions.
All inputs are finite; a program needn't handle non-finite values.
Results may differ from the reference program's by a relative error of at most 0.0015.
Values may be sent and summed in bfloat16 or wider, within the bound.
No kernel may reach another device: no remote copies, remote signals or barrier semaphores. Data moves between devices by JAX's collectives and lax.ppermute only.
A program may use at most 128 MiB of HBM per device.

```python
import math
import jax
import jax.numpy as jnp
import numpy as np
from jax import lax

B = 512
KB = 6
CAP = 2
NB = 96
N_DP = 16
N_OPT = 8


def symmetric_draw(key, low, high, spread):
    key_noise, key_diagonal = jax.random.split(key)
    noise_part = jnp.clip(jax.random.normal(key_noise, (N_DP, N_OPT, CAP, B, B), jnp.float32), -5.0, 5.0)
    off_part = spread * 0.5 * (noise_part + jnp.swapaxes(noise_part, -1, -2))
    diagonal_part = jax.random.uniform(key_diagonal, (N_DP, N_OPT, CAP, B, 1), jnp.float32, minval=low, maxval=high)
    identity = jnp.eye(B, dtype=jnp.float32)
    return off_part * (1.0 - identity) + diagonal_part * identity


def draw_grad_partial(key, part):
    key = jax.random.fold_in(key, 5)
    key_rows = jax.random.fold_in(key, 0)
    key_cols = jax.random.fold_in(key, 1)
    key_noise = jax.random.fold_in(key, 3)
    row_scale = jnp.exp(jax.random.uniform(key_rows, (NB, B, 1), jnp.float32, minval=0.0, maxval=math.log(10.0)))
    row_rise = 1.0 + 2.0 * jnp.arange(B, dtype=jnp.float32)[None, :, None] / (B - 1)
    col_scale = jnp.exp(jax.random.uniform(key_cols, (NB, 1, B), jnp.float32, minval=0.0, maxval=math.log(10.0)))
    draw_base = jnp.clip(jax.random.normal(key_noise, (N_DP, NB, B, B), jnp.float32), -6.0, 6.0)
    return (0.005 * draw_base * row_scale * row_rise * col_scale).astype(jnp.bfloat16)


def moment_rows(key, lowest, rise_top):
    row_rise = jnp.exp(math.log(rise_top) * jnp.arange(B, dtype=jnp.float32)[None, :, None] / (B - 1))
    base = jnp.exp(jax.random.uniform(key, (NB, B, B), jnp.float32, minval=math.log(lowest), maxval=0.0))
    return base * row_rise


def draw_second_moment(key, part):
    key = jax.random.fold_in(key, 7)
    return moment_rows(key, 0.01, 300.0)


def draw_factor_left(key, part):
    key = jax.random.fold_in(key, 11)
    return symmetric_draw(key, 0.3, 2.0, 0.03)


def draw_factor_right(key, part):
    key = jax.random.fold_in(key, 12)
    return symmetric_draw(key, 0.3, 2.0, 0.03)


def draw_root_left(key, part):
    key = jax.random.fold_in(key, 13)
    return symmetric_draw(key, 0.5, 1.5, 0.02).astype(jnp.bfloat16)


def draw_root_right(key, part):
    key = jax.random.fold_in(key, 14)
    return symmetric_draw(key, 0.5, 1.5, 0.02).astype(jnp.bfloat16)


def levels(own_key, shape, cuts, low, high):
    loudness = 1.0
    for axis_at, parts in cuts:
        heights = jax.random.uniform(jax.random.fold_in(jax.random.fold_in(own_key, 6), axis_at), (parts,), jnp.float32, low / len(cuts), high / len(cuts))
        loudness = loudness * jnp.repeat(jnp.exp(heights), shape[axis_at] // parts).reshape((-1,) + (1,) * (len(shape) - 1 - axis_at))
    return loudness


def deal_out(stream_key, own, number, rows, amount, top, bound, slope):
    order = jax.random.permutation(stream_key, amount)
    packed, ordinary = portions_of(amount, rows * top, bound, slope, True), portions_of(amount, rows * top, bound, slope, False)
    places = jnp.arange(amount)

    def named(sizes, offset_by):
        used = int((sizes > 0).sum())
        fixed = max(1, used // 4)
        passed = fixed + (places - fixed + offset_by * (used - fixed)) % max(1, amount - fixed)
        return jnp.zeros((amount,), jnp.int32).at[order[jnp.where(places < fixed, places, passed)]].set(jnp.asarray(sizes, jnp.int32))

    sizes = jnp.where(number % 4 == 0, named(packed, number // 4), named(ordinary, number - number // 4 - 1))
    mixed = jax.random.permutation(jax.random.fold_in(own, 3), amount)
    source_of, receiver = mixed[0:amount // 2 * 2:2], mixed[1:amount // 2 * 2:2]
    margin = jnp.minimum(sizes[source_of] - 1, bound - sizes[receiver]) // 2
    margin = jnp.where((source_of == order[0]) | (receiver == order[0]) | (sizes[receiver] == 0), 0, jnp.maximum(margin, 0))
    passed = jax.random.randint(jax.random.fold_in(own, 4), (amount // 2,), 0, 1 << 20) % (margin + 1)
    sizes = sizes.at[source_of].add(-passed).at[receiver].add(passed)
    labels = jnp.searchsorted(jnp.cumsum(sizes), jnp.arange(rows * top), side="right").astype(jnp.int32)
    table = labels.reshape(top, rows).T
    table = table[jax.random.permutation(jax.random.fold_in(own, 1), rows)]
    offset_by = jax.random.randint(jax.random.fold_in(own, 2), (rows, 1), 0, top)
    return jnp.take_along_axis(table, (jnp.arange(top)[None, :] + offset_by) % top, axis=1)


def portions_of(count, total, most, skew, full):
    portions = [(1 << 20) // math.isqrt(rank ** skew) + 1 for rank in range(1, count + 1)]
    largest = most if full else min(most, max(-(-total // count), total * portions[0] // sum(portions)))
    least = 1 if total - largest >= count - 1 else 0
    given, rest = [largest] + [least] * (count - 1), total - largest - least * (count - 1)
    while rest > 0:
        candidates = [i for i in range(1, count) if given[i] < largest] or [i for i in range(1, count) if given[i] < most]
        mass, left = sum([portions[i] for i in candidates]), rest
        for i in candidates:
            more = min(most - given[i], max(1, left * portions[i] // mass), rest)
            given[i] = given[i] + more
            rest = rest - more
    return np.array(given)


def centred(own_key, dims, scale, bound, shards=(), kind=jnp.bfloat16):
    array = scale * jax.random.normal(own_key, dims, jnp.float32)
    if shards:
        array = array * levels(own_key, dims, shards, -0.22, 0.18)
    return jnp.clip(array, -bound, bound).astype(kind)


def setup_inputs(seed: int = 0) -> dict:
    key_of = jax.random.split(jax.random.key(seed), 9)
    grad_partial = draw_grad_partial(jax.random.fold_in(key_of[8], 71), 0)
    master = centred(key_of[1], (NB, B, B), 1.0, 6.0, ((0, 16), (1, 8)), jnp.float32)
    second_moment = draw_second_moment(jax.random.fold_in(key_of[8], 71), 0)
    owner_table_keys = jax.random.split(jax.random.fold_in(key_of[3], 1), NB // KB)
    owner_table_turns = jax.random.permutation(jax.random.fold_in(key_of[3], 3), NB // KB)
    owner_table = jax.vmap(lambda own, number: deal_out(jax.random.fold_in(key_of[3], 2), own, number, KB, N_OPT, 1, CAP, 2))(owner_table_keys, owner_table_turns).reshape((NB, 1))
    factor_left = draw_factor_left(jax.random.fold_in(key_of[8], 71), 0)
    factor_right = draw_factor_right(jax.random.fold_in(key_of[8], 71), 0)
    root_left = draw_root_left(jax.random.fold_in(key_of[8], 71), 0)
    root_right = draw_root_right(jax.random.fold_in(key_of[8], 71), 0)
    return dict(grad_partial=grad_partial, master=master, second_moment=second_moment, owner_table=owner_table, factor_left=factor_left, factor_right=factor_right, root_left=root_left, root_right=root_right)


BETA_FACTOR = 0.75
BETA_MOMENT = 0.95
LEARN_RATE = 0.1
EPS_ADAM = 1e-08
EPS_GRAFT = 1e-06

def block_work(operands):
    block_grad, left_root, right_root = operands
    gram_left = jnp.dot(block_grad, block_grad.T, precision=lax.Precision.HIGHEST) / B
    gram_right = jnp.dot(block_grad.T, block_grad, precision=lax.Precision.HIGHEST) / B
    half_product = jnp.dot(left_root, block_grad.astype(jnp.bfloat16), preferred_element_type=jnp.float32).astype(jnp.bfloat16)
    direction = jnp.dot(half_product, right_root, preferred_element_type=jnp.float32)
    return (gram_left, gram_right, direction)

def reference(grad_partial, master, second_moment, owner_table, factor_left, factor_right, root_left, root_right):

    def add_replica(replica, running):
        return running + grad_partial[replica].astype(jnp.float32)
    summed_grad = lax.fori_loop(0, N_DP, add_replica, jnp.zeros((NB, B, B), jnp.float32))
    owner_rows = owner_table[:, 0].reshape(N_DP, KB)
    position = jnp.arange(KB)
    same_owner = owner_rows[:, :, None] == owner_rows[:, None, :]
    earlier = position[None, :] < position[:, None]
    slot_rank = lax.optimization_barrier(jnp.sum((same_owner & earlier[None]).astype(jnp.int32), axis=2))
    row_index = jnp.arange(N_DP).astype(jnp.int32)[:, None]
    left_roots = root_left[row_index, owner_rows, slot_rank].reshape(NB, B, B)
    right_roots = root_right[row_index, owner_rows, slot_rank].reshape(NB, B, B)
    gram_left, gram_right, direction = lax.map(block_work, (summed_grad, left_roots, right_roots))
    left_states = factor_left[row_index, owner_rows, slot_rank]
    right_states = factor_right[row_index, owner_rows, slot_rank]
    left_block = BETA_FACTOR * left_states + (1.0 - BETA_FACTOR) * gram_left.reshape(N_DP, KB, B, B)
    right_block = BETA_FACTOR * right_states + (1.0 - BETA_FACTOR) * gram_right.reshape(N_DP, KB, B, B)
    left_new = factor_left.at[row_index, owner_rows, slot_rank].set(left_block)
    right_new = factor_right.at[row_index, owner_rows, slot_rank].set(right_block)
    moment_new = BETA_MOMENT * second_moment + (1.0 - BETA_MOMENT) * summed_grad * summed_grad
    adam_step = summed_grad / (jnp.sqrt(moment_new) + EPS_ADAM)
    adam_square = lax.optimization_barrier(jnp.sum(adam_step * adam_step, axis=(1, 2)))
    direction_square = lax.optimization_barrier(jnp.sum(direction * direction, axis=(1, 2)))
    graft_scale = jnp.sqrt(adam_square) / (jnp.sqrt(direction_square) + EPS_GRAFT)
    master_new = master - LEARN_RATE * graft_scale[:, None, None] * direction
    weights = master_new.astype(jnp.bfloat16)
    return (master_new, moment_new, weights, left_new, right_new)
```

```python
import functools

import jax
import jax.numpy as jnp
from jax import lax
from jax.experimental import pallas as pl
from jax.experimental.pallas import tpu as pltpu
from jax.sharding import PartitionSpec as P

BETA_FACTOR = 0.75
BETA_MOMENT = 0.95
LEARN_RATE = 0.1
EPS_ADAM = 1e-08
EPS_GRAFT = 1e-06
SIDE = 4
CHUNKS = ((0, 3), (3, 6))
VMEM = 60 * 2**20


def shift_perm(axis, step):
    pairs = []
    for z in range(SIDE):
        for y in range(SIDE):
            to_z = (z + step) % SIDE if axis == "z" else z
            to_y = (y + step) % SIDE if axis == "y" else y
            pairs.append((z * SIDE + y, to_z * SIDE + to_y))
    return pairs


def send(value, axis, step):
    return lax.ppermute(value, "dp", shift_perm(axis, step))


def after(value, *earlier):
    return lax.optimization_barrier((value,) + earlier)[0]


ORDER = (("y", 1), ("z", 1), ("y", 3), ("z", 3), ("y", 2), ("z", 2))
OTHER = {"y": "z", "z": "y"}


def exchange(make):
    got = {}
    for axis, step in ORDER:
        value = make(axis, step)
        got[axis, step] = send(after(value, got["z", 1]) if (axis, step) == ORDER[-1] else value, axis, step)
    return got


def together(got):
    return dict(zip(got, lax.optimization_barrier(tuple(got.values()))))


def sum_replicas(parts, place, needed):
    blocks, half_rows, width = parts.shape[2], parts.shape[3] // 2, parts.shape[4]
    top = {"y": 0, "z": half_rows}

    def raw(axis, step):
        at = (place[axis] + step) % SIDE
        start = (0, at, 0, top[axis], 0) if axis == "y" else (at, 0, 0, top[axis], 0)
        size = (SIDE, 1) if axis == "y" else (1, SIDE)
        got = lax.dynamic_slice(parts, start, size + (blocks, half_rows, width))
        return got.reshape((SIDE, blocks, half_rows, width))

    near = together(exchange(raw))

    def total(chunk, axis, step):
        first, last = chunk
        at = (place[axis] + step) % SIDE
        axis = OTHER[axis]
        start = (at, place["y"]) if axis == "y" else (place["z"], at)
        size = (last - first, half_rows, width)
        own = lax.dynamic_slice(parts, start + (first, top[axis], 0), (1, 1) + size)[0, 0]
        picked = [lax.dynamic_slice(near[axis, hop], (at, first, 0, 0), (1,) + size)[0] for hop in (1, 3, 2)]
        own, one, three, two = [part.astype(jnp.float32) for part in [own] + picked]
        return (own + one) + (three + two)

    parcels = []
    for number, chunk in enumerate(CHUNKS):
        make = functools.partial(total, chunk)
        if parcels:
            behind = parcels[-1][2]
            far = exchange(lambda axis, step: after(make(axis, step), behind))
        else:
            far = exchange(make)
        far = together(far)
        halves = []
        for axis in ("y", "z"):
            one, three, two = [far[OTHER[axis], step] for step in (1, 3, 2)]
            halves.append((total(chunk, OTHER[axis], 0) + one) + (after(three, *needed[number]) + two))
        grad = jnp.concatenate(halves, axis=1)
        rounded = lax.reduce_precision(grad, 8, 7)
        parcels.append((grad, rounded, rounded.astype(jnp.bfloat16)))
    return parcels


def place_kernel(step, first, place_ref, upper_ref, lower_ref, *refs):
    out, sems = refs[-2:]
    z, y = place_ref[0], place_ref[1]
    still_z, still_y = lax.rem(z + SIDE - step, SIDE), lax.rem(y + SIDE - step, SIDE)
    blocks, rows = pl.ds(first, upper_ref.shape[1]), upper_ref.shape[2]
    copies = []
    for hop in range(SIDE):
        upper = out.at[still_z, lax.rem(y + SIDE - hop, SIDE), blocks, pl.ds(0, rows)]
        lower = out.at[lax.rem(z + SIDE - hop, SIDE), still_y, blocks, pl.ds(rows, rows)]
        copies.append(pltpu.make_async_copy(upper_ref.at[hop], upper, sems.at[hop]))
        copies.append(pltpu.make_async_copy(lower_ref.at[hop], lower, sems.at[SIDE + hop]))
    for copy in copies:
        copy.start()
    for copy in copies:
        copy.wait()


def put(out, shape, place, step, upper, lower, first):
    spot = jnp.stack([place["z"], place["y"]]).astype(jnp.int32)
    before = [] if out is None else [out]
    piece = pl.BlockSpec(upper.shape, lambda t: (0, 0, 0, 0))
    return pl.pallas_call(
        functools.partial(place_kernel, step, first),
        grid=(1,),
        out_shape=jax.ShapeDtypeStruct(shape, jnp.bfloat16),
        in_specs=[pl.BlockSpec(memory_space=pltpu.SMEM)]
        + [piece, piece]
        + [pl.BlockSpec(memory_space=pl.ANY)] * len(before),
        out_specs=pl.BlockSpec(memory_space=pl.ANY),
        scratch_shapes=[pltpu.SemaphoreType.DMA((2 * SIDE,))],
        input_output_aliases={3: 0} if before else {},
        compiler_params=pltpu.CompilerParams(vmem_limit_bytes=8 * 2**20),
        cost_estimate=pl.CostEstimate(flops=0, bytes_accessed=8 * upper.size, transcendentals=0),
        name="place_weights",
    )(spot, upper, lower, *before)


def direction_kernel(owner_ref, rank_ref, left_ref, grad_ref, right_ref, out_ref, square_ref):
    width = right_ref.shape[-1]
    grad = grad_ref[...].reshape(width, width)
    half = jnp.dot(left_ref[0, 0], grad, preferred_element_type=jnp.float32).astype(jnp.bfloat16)
    rows = jnp.dot(half, right_ref[0, 0], preferred_element_type=jnp.float32)
    out_ref[0] = rows
    square_ref[...] = jnp.full(square_ref.shape, jnp.sum(rows * rows), jnp.float32)


def directions(owner, rank, left_rows, grad_whole, right_roots):
    opt_count, blocks, slab_rows, width = grad_whole.shape
    grid_spec = pltpu.PrefetchScalarGridSpec(
        num_scalar_prefetch=2,
        grid=(blocks,),
        in_specs=[
            pl.BlockSpec((1, 1, slab_rows, width), lambda k, owner, rank: (rank[k], owner[k], 0, 0)),
            pl.BlockSpec((opt_count, 1, slab_rows, width), lambda k, owner, rank: (0, k, 0, 0)),
            pl.BlockSpec((1, 1, width, width), lambda k, owner, rank: (owner[k], rank[k], 0, 0)),
        ],
        out_specs=[
            pl.BlockSpec((1, slab_rows, width), lambda k, owner, rank: (k, 0, 0)),
            pl.BlockSpec((1, 8, 128), lambda k, owner, rank: (k, 0, 0)),
        ],
    )
    flops = blocks * 4 * slab_rows * width * width
    return pl.pallas_call(
        direction_kernel,
        grid_spec=grid_spec,
        out_shape=[
            jax.ShapeDtypeStruct((blocks, slab_rows, width), jnp.float32),
            jax.ShapeDtypeStruct((blocks, 8, 128), jnp.float32),
        ],
        compiler_params=pltpu.CompilerParams(vmem_limit_bytes=VMEM),
        cost_estimate=pl.CostEstimate(
            flops=flops, bytes_accessed=blocks * width * width * 4, transcendentals=0
        ),
        name="directions",
    )(owner, rank, left_rows, grad_whole, right_roots)


def gram_kernel(block_ref, used_ref, *refs):
    highs = refs[: len(CHUNKS)]
    low_ref, left_ref, right_ref, left_out, right_out, high_ref = refs[len(CHUNKS) :]
    slot = pl.program_id(0)
    width = left_ref.shape[-1]
    for number, (first, last) in enumerate(CHUNKS):

        @pl.when((block_ref[slot] >= first) & (block_ref[slot] < last))
        def _():
            high_ref[...] = highs[number][...].reshape(width, width)

    @pl.when(used_ref[slot] == 1)
    def _():
        high = high_ref[...]
        low = low_ref[...].reshape(width, width)
        scale = (1.0 - BETA_FACTOR) / width

        def gram(dims):
            dot = functools.partial(
                lax.dot_general, dimension_numbers=(dims, ((), ())), preferred_element_type=jnp.float32
            )
            cross = dot(high, low)
            return dot(high, high) + (cross + cross.T)

        left_out[0, 0, 0] = BETA_FACTOR * left_ref[0, 0, 0] + scale * gram(((1,), (1,)))
        right_out[0, 0, 0] = BETA_FACTOR * right_ref[0, 0, 0] + scale * gram(((0,), (0,)))

    @pl.when(used_ref[slot] == 0)
    def _():
        left_out[...] = left_ref[...]
        right_out[...] = right_ref[...]


def factors(block_at, used, highs, low, factor_left, factor_right):
    slot_count, width = factor_left.shape[2], factor_left.shape[-1]
    opt_count, _, slab_rows, _ = low.shape

    def grad_spec(first, last):
        def at_block(s, at, used):
            return (0, jnp.clip(at[s] - first, 0, last - first - 1), 0, 0)

        return pl.BlockSpec((opt_count, 1, slab_rows, width), at_block)

    state_spec = pl.BlockSpec((1, 1, 1, width, width), lambda s, at, used: (0, 0, s, 0, 0))
    grid_spec = pltpu.PrefetchScalarGridSpec(
        num_scalar_prefetch=2,
        grid=(slot_count,),
        in_specs=[grad_spec(*chunk) for chunk in CHUNKS]
        + [grad_spec(0, CHUNKS[-1][1]), state_spec, state_spec],
        out_specs=[state_spec, state_spec],
        scratch_shapes=[pltpu.VMEM((width, width), jnp.bfloat16)],
    )
    return pl.pallas_call(
        gram_kernel,
        grid_spec=grid_spec,
        out_shape=[jax.ShapeDtypeStruct(factor_left.shape, jnp.float32)] * 2,
        compiler_params=pltpu.CompilerParams(vmem_limit_bytes=VMEM),
        cost_estimate=pl.CostEstimate(
            flops=slot_count * 12 * width**3,
            bytes_accessed=slot_count * 20 * width * width,
            transcendentals=0,
        ),
        name="factors",
    )(block_at, used, *highs, low, factor_left, factor_right)


def spread_weights(weights):
    half_rows = weights.shape[1] // 2
    own = {"y": weights[:, :half_rows], "z": weights[:, half_rows:]}
    near = exchange(lambda axis, step: own[axis])
    begun = near["y", 1]
    near = together(near)
    line = {axis: jnp.stack([own[axis]] + [near[axis, hop] for hop in (1, 2, 3)]) for axis in own}
    return begun, line, exchange(lambda axis, step: line[OTHER[axis]])


def put_all(out, shape, place, line, far, first):
    out = put(out, shape, place, 0, line["y"], line["z"], first)
    for step in (1, 3, 2):
        out = put(out, shape, place, step, far["z", step], far["y", step], first)
    return out


def shards(
    grad_partial,
    master,
    second_moment,
    owner_table,
    factor_left,
    factor_right,
    root_left,
    root_right,
):
    opt_count = lax.axis_size("opt")
    slot_count = factor_left.shape[2]
    row_blocks, slab_rows, width = master.shape
    dp_at, opt_at = lax.axis_index("dp"), lax.axis_index("opt")
    place = {"z": dp_at // SIDE, "y": dp_at % SIDE}

    owner = lax.dynamic_slice_in_dim(owner_table[:, 0], dp_at * row_blocks, row_blocks, 0)
    position = jnp.arange(row_blocks)
    same_owner = owner[:, None] == owner[None, :]
    earlier = position[None, :] < position[:, None]
    rank = jnp.sum((same_owner & earlier).astype(jnp.int32), axis=1)
    mine = (owner[None, :] == opt_at) & (rank[None, :] == jnp.arange(slot_count)[:, None])
    used = jnp.sum(mine.astype(jnp.int32), axis=1)
    block_at = jnp.sum(jnp.where(mine, position[None, :], 0), axis=1).astype(jnp.int32)

    right_roots = lax.all_gather(root_right[0, 0], "opt", axis=0)
    left_rows = lax.all_to_all(
        root_left[0, 0].reshape(slot_count, opt_count, slab_rows, width),
        "opt",
        split_axis=1,
        concat_axis=1,
        tiled=True,
    )

    parts = grad_partial[0].reshape(SIDE, SIDE, row_blocks, slab_rows, width)
    parcels = sum_replicas(parts, place, ((left_rows, right_roots), ()))

    lows, wholes, masters, moments, sent = [], [], [], [], []
    for number, (first, last) in enumerate(CHUNKS):
        grad, rounded, high = parcels[number]
        lows.append((grad - rounded).astype(jnp.bfloat16))
        if number > 0:
            high = after(high, wholes[-1])
        wholes.append(lax.all_gather(high, "opt", axis=0))
        moment = BETA_MOMENT * second_moment[first:last] + (1.0 - BETA_MOMENT) * grad * grad
        step = grad / (jnp.sqrt(moment) + EPS_ADAM)
        adam_square = jnp.sum(step * step, axis=(1, 2))
        whole = wholes[number] if number == 0 else after(wholes[number], sent[0][0])
        rows, row_square = directions(owner[first:last], rank[first:last], left_rows, whole, right_roots)
        squares = jnp.concatenate(
            [jnp.broadcast_to(adam_square[:, None, None], row_square.shape), row_square], axis=0
        )
        squares = jnp.broadcast_to(squares[None], (opt_count,) + squares.shape)
        squares = lax.all_to_all(squares, "opt", split_axis=0, concat_axis=0, tiled=True)
        if number > 0:
            squares = after(squares, *[sent[0][2][key] for key in ORDER[:4]])
        adam_total, row_total = jnp.split(jnp.sum(squares, axis=0)[:, 0, 0], 2)
        graft_scale = jnp.sqrt(adam_total) / (jnp.sqrt(row_total) + EPS_GRAFT)
        fresh = master[first:last] - LEARN_RATE * graft_scale[:, None, None] * rows
        sent.append(spread_weights(fresh.astype(jnp.bfloat16)))
        masters.append(fresh)
        moments.append(moment)

    low_whole = lax.all_gather(after(jnp.concatenate(lows), squares), "opt", axis=0)
    left_new, right_new = factors(block_at, used, wholes, low_whole, factor_left, factor_right)
    sent[0][1]["y"] = after(sent[0][1]["y"], sent[1][2]["y", 1])
    gathered = put_all(None, parts.shape, place, *sent[0][1:], 0)
    sent[1][1]["y"] = after(sent[1][1]["y"], left_new)
    gathered = put_all(gathered, parts.shape, place, *sent[1][1:], CHUNKS[1][0])
    return (
        jnp.concatenate(masters, axis=0),
        jnp.concatenate(moments, axis=0),
        gathered.reshape(-1, slab_rows, width),
        left_new,
        right_new,
    )


def solution(mesh):
    placed = (
        P("dp", None, "opt", None),
        P("dp", "opt", None),
        P("dp", "opt", None),
        P(),
        P("dp", "opt", None, None, None),
        P("dp", "opt", None, None, None),
        P("dp", "opt", None, None, None),
        P("dp", "opt", None, None, None),
    )
    return jax.shard_map(
        shards,
        mesh=mesh,
        in_specs=placed,
        out_specs=(
            P("dp", "opt", None),
            P("dp", "opt", None),
            P(None, "opt", None),
            P("dp", "opt", None, None, None),
            P("dp", "opt", None, None, None),
        ),
        check_vma=False,
    )
```

```python
import functools

import jax
import jax.numpy as jnp
from jax import lax
from jax.experimental import pallas as pl
from jax.experimental.pallas import tpu as pltpu
from jax.sharding import PartitionSpec as P

BETA_FACTOR = 0.75
BETA_MOMENT = 0.95
LEARN_RATE = 0.1
EPS_ADAM = 1e-08
EPS_GRAFT = 1e-06
SIDE = 4
VMEM = 60 * 2**20


def shift_perm(axis, step):
    pairs = []
    for z in range(SIDE):
        for y in range(SIDE):
            to_z = (z + step) % SIDE if axis == "z" else z
            to_y = (y + step) % SIDE if axis == "y" else y
            pairs.append((z * SIDE + y, to_z * SIDE + to_y))
    return pairs


def send(value, axis, step):
    return lax.ppermute(value, "dp", shift_perm(axis, step))


def after(value, *earlier):
    return lax.optimization_barrier((value,) + earlier)[0]


ORDER = (("y", 1), ("z", 1), ("y", 3), ("z", 3), ("y", 2), ("z", 2))
OTHER = {"y": "z", "z": "y"}


def exchange(make):
    got = {}
    for axis, step in ORDER:
        value = make(axis, step)
        got[axis, step] = send(after(value, got["z", 1]) if (axis, step) == ORDER[-1] else value, axis, step)
    return got


def together(got):
    return dict(zip(got, lax.optimization_barrier(tuple(got.values()))))


def sum_replicas(parts, place, needed):
    blocks, half_rows, width = parts.shape[2], parts.shape[3] // 2, parts.shape[4]
    top = {"y": 0, "z": half_rows}

    def raw(axis, step):
        at = (place[axis] + step) % SIDE
        start = (0, at, 0, top[axis], 0) if axis == "y" else (at, 0, 0, top[axis], 0)
        size = (SIDE, 1) if axis == "y" else (1, SIDE)
        got = lax.dynamic_slice(parts, start, size + (blocks, half_rows, width))
        return got.reshape((SIDE, blocks, half_rows, width))

    near = together(exchange(raw))

    def total(axis, step):
        at = (place[axis] + step) % SIDE
        axis = OTHER[axis]
        start = (at, place["y"]) if axis == "y" else (place["z"], at)
        own = lax.dynamic_slice(parts, start + (0, top[axis], 0), (1, 1, blocks, half_rows, width))[0, 0]
        picked = [lax.dynamic_index_in_dim(near[axis, hop], at, 0, keepdims=False) for hop in (1, 3, 2)]
        own, one, three, two = [part.astype(jnp.float32) for part in [own] + picked]
        return (own + one) + (three + two)

    far = together(exchange(total))
    halves = []
    for axis in ("y", "z"):
        one, three, two = [far[OTHER[axis], step] for step in (1, 3, 2)]
        halves.append((total(OTHER[axis], 0) + one) + (after(three, *needed) + two))
    return jnp.concatenate(halves, axis=1)


def place_kernel(step, place_ref, *refs):
    out, sems = refs[-2:]
    pieces = refs[:-2]
    z, y = place_ref[0], place_ref[1]
    still_z, still_y = lax.rem(z + SIDE - step, SIDE), lax.rem(y + SIDE - step, SIDE)
    count = pieces[0].shape[0]
    rows = pieces[0].shape[2]
    copies = []
    for hop in range(SIDE):
        upper = out.at[still_z, lax.rem(y + SIDE - hop, SIDE), :, pl.ds(0, rows)]
        lower = out.at[lax.rem(z + SIDE - hop, SIDE), still_y, :, pl.ds(rows, rows)]
        for half, target in enumerate((upper, lower)):
            source = pieces[half * (SIDE // count) + hop // count].at[hop % count]
            copies.append(pltpu.make_async_copy(source, target, sems.at[half * SIDE + hop]))
    for copy in copies:
        copy.start()
    for copy in copies:
        copy.wait()


def put(out, shape, place, step, upper, lower):
    spot = jnp.stack([place["z"], place["y"]]).astype(jnp.int32)
    before = [] if out is None else [out]
    pieces = upper + lower
    piece = pl.BlockSpec(pieces[0].shape, lambda t: (0, 0, 0, 0))

    def kernel(place_ref, *refs):
        place_kernel(step, place_ref, *refs[: len(pieces)], *refs[-2:])

    return pl.pallas_call(
        kernel,
        grid=(1,),
        out_shape=jax.ShapeDtypeStruct(shape, jnp.bfloat16),
        in_specs=[pl.BlockSpec(memory_space=pltpu.SMEM)]
        + [piece] * len(pieces)
        + [pl.BlockSpec(memory_space=pl.ANY)] * len(before),
        out_specs=pl.BlockSpec(memory_space=pl.ANY),
        scratch_shapes=[pltpu.SemaphoreType.DMA((2 * SIDE,))],
        input_output_aliases={1 + len(pieces): 0} if before else {},
        compiler_params=pltpu.CompilerParams(vmem_limit_bytes=8 * 2**20),
        cost_estimate=pl.CostEstimate(
            flops=0, bytes_accessed=4 * sum(value.size for value in pieces), transcendentals=0
        ),
        name="place_weights",
    )(spot, *pieces, *before)


def direction_kernel(owner_ref, rank_ref, left_ref, grad_ref, right_ref, adam_ref, out_ref, square_ref):
    k = pl.program_id(0)
    width = right_ref.shape[-1]
    grad = grad_ref[...].reshape(width, width)
    half = jnp.dot(left_ref[0, 0], grad, preferred_element_type=jnp.float32).astype(jnp.bfloat16)
    rows = jnp.dot(half, right_ref[0, 0], preferred_element_type=jnp.float32)
    out_ref[0] = rows

    @pl.when(k == 0)
    def _():
        square_ref[...] = adam_ref[...]

    lane = lax.broadcasted_iota(jnp.int32, square_ref.shape, 1)
    square_ref[...] += jnp.where(lane == k, jnp.sum(rows * rows), 0.0)


def directions(owner, rank, left_rows, grad_whole, right_roots, adam_square):
    opt_count, blocks, slab_rows, width = grad_whole.shape
    grid_spec = pltpu.PrefetchScalarGridSpec(
        num_scalar_prefetch=2,
        grid=(blocks,),
        in_specs=[
            pl.BlockSpec((1, 1, slab_rows, width), lambda k, owner, rank: (rank[k], owner[k], 0, 0)),
            pl.BlockSpec((opt_count, 1, slab_rows, width), lambda k, owner, rank: (0, k, 0, 0)),
            pl.BlockSpec((1, 1, width, width), lambda k, owner, rank: (owner[k], rank[k], 0, 0)),
            pl.BlockSpec((8, 128), lambda k, owner, rank: (0, 0)),
        ],
        out_specs=[
            pl.BlockSpec((1, slab_rows, width), lambda k, owner, rank: (k, 0, 0)),
            pl.BlockSpec((8, 128), lambda k, owner, rank: (0, 0)),
        ],
    )
    flops = blocks * 4 * slab_rows * width * width
    return pl.pallas_call(
        direction_kernel,
        grid_spec=grid_spec,
        out_shape=[
            jax.ShapeDtypeStruct((blocks, slab_rows, width), jnp.float32),
            jax.ShapeDtypeStruct((8, 128), jnp.float32),
        ],
        compiler_params=pltpu.CompilerParams(vmem_limit_bytes=VMEM),
        cost_estimate=pl.CostEstimate(
            flops=flops, bytes_accessed=blocks * width * width * 4, transcendentals=0
        ),
        name="directions",
    )(owner, rank, left_rows, grad_whole, right_roots, adam_square)


def gram_kernel(block_ref, used_ref, high_ref, low_ref, left_ref, right_ref, left_out, right_out):
    slot = pl.program_id(0)
    width = left_ref.shape[-1]

    @pl.when(used_ref[slot] == 1)
    def _():
        high = high_ref[...].reshape(width, width)
        low = low_ref[...].reshape(width, width)
        scale = (1.0 - BETA_FACTOR) / width

        def gram(dims):
            dot = functools.partial(
                lax.dot_general, dimension_numbers=(dims, ((), ())), preferred_element_type=jnp.float32
            )
            cross = dot(high, low)
            return dot(high, high) + (cross + cross.T)

        left_out[0, 0, 0] = BETA_FACTOR * left_ref[0, 0, 0] + scale * gram(((1,), (1,)))
        right_out[0, 0, 0] = BETA_FACTOR * right_ref[0, 0, 0] + scale * gram(((0,), (0,)))

    @pl.when(used_ref[slot] == 0)
    def _():
        left_out[...] = left_ref[...]
        right_out[...] = right_ref[...]


def factors(block_at, used, high, low, factor_left, factor_right):
    slot_count, width = factor_left.shape[2], factor_left.shape[-1]
    opt_count, _, slab_rows, _ = high.shape
    grad_spec = pl.BlockSpec((opt_count, 1, slab_rows, width), lambda s, at, used: (0, at[s], 0, 0))
    state_spec = pl.BlockSpec((1, 1, 1, width, width), lambda s, at, used: (0, 0, s, 0, 0))
    grid_spec = pltpu.PrefetchScalarGridSpec(
        num_scalar_prefetch=2,
        grid=(slot_count,),
        in_specs=[grad_spec, grad_spec, state_spec, state_spec],
        out_specs=[state_spec, state_spec],
    )
    return pl.pallas_call(
        gram_kernel,
        grid_spec=grid_spec,
        out_shape=[jax.ShapeDtypeStruct(factor_left.shape, jnp.float32)] * 2,
        compiler_params=pltpu.CompilerParams(vmem_limit_bytes=VMEM),
        cost_estimate=pl.CostEstimate(
            flops=slot_count * 12 * width**3,
            bytes_accessed=slot_count * 20 * width * width,
            transcendentals=0,
        ),
        name="factors",
    )(block_at, used, high, low, factor_left, factor_right)


def gather_weights(weights, shape, place, meanwhile):
    half_rows = weights.shape[1] // 2
    own = {"y": weights[:, :half_rows], "z": weights[:, half_rows:]}
    near = together(exchange(lambda axis, step: own[axis]))
    line = {axis: jnp.stack([own[axis]] + [near[axis, hop] for hop in (1, 2, 3)]) for axis in own}
    far = {(axis, step): send(line[OTHER[axis]], axis, step) for axis, step in ORDER[:4]}
    for axis in ("y", "z"):
        halves = [send(far[axis, 1][:2], axis, 1), send(far[axis, 3][2:], axis, 3)]
        far[axis, 2] = halves
    out = put(None, shape, place, 0, [line["y"]], [line["z"]])
    out = put(out, shape, place, 1, [far["z", 1]], [far["y", 1]])
    far["z", 3] = after(far["z", 3], meanwhile)
    out = put(out, shape, place, 3, [far["z", 3]], [far["y", 3]])
    return put(out, shape, place, 2, far["z", 2], far["y", 2])


def shards(
    grad_partial,
    master,
    second_moment,
    owner_table,
    factor_left,
    factor_right,
    root_left,
    root_right,
):
    opt_count = lax.axis_size("opt")
    slot_count = factor_left.shape[2]
    row_blocks, slab_rows, width = master.shape
    dp_at, opt_at = lax.axis_index("dp"), lax.axis_index("opt")
    place = {"z": dp_at // SIDE, "y": dp_at % SIDE}

    owner = lax.dynamic_slice_in_dim(owner_table[:, 0], dp_at * row_blocks, row_blocks, 0)
    position = jnp.arange(row_blocks)
    same_owner = owner[:, None] == owner[None, :]
    earlier = position[None, :] < position[:, None]
    rank = jnp.sum((same_owner & earlier).astype(jnp.int32), axis=1)
    mine = (owner[None, :] == opt_at) & (rank[None, :] == jnp.arange(slot_count)[:, None])
    used = jnp.sum(mine.astype(jnp.int32), axis=1)
    block_at = jnp.sum(jnp.where(mine, position[None, :], 0), axis=1).astype(jnp.int32)

    right_roots = lax.all_gather(root_right[0, 0], "opt", axis=0)
    left_rows = lax.all_to_all(
        root_left[0, 0].reshape(slot_count, opt_count, slab_rows, width),
        "opt",
        split_axis=1,
        concat_axis=1,
        tiled=True,
    )

    parts = grad_partial[0].reshape(SIDE, SIDE, row_blocks, slab_rows, width)
    grad = sum_replicas(parts, place, (left_rows, right_roots))

    rounded = lax.reduce_precision(grad, 8, 7)
    high = rounded.astype(jnp.bfloat16)
    high_whole = lax.all_gather(high, "opt", axis=0)
    moment_new = BETA_MOMENT * second_moment + (1.0 - BETA_MOMENT) * grad * grad
    step = grad / (jnp.sqrt(moment_new) + EPS_ADAM)
    adam_square = jnp.sum(step * step, axis=(1, 2))
    adam_tile = jnp.pad(adam_square[None], ((0, 7), (64, 64 - row_blocks)))
    rows, squares = directions(owner, rank, left_rows, high_whole, right_roots, adam_tile)
    squares = jnp.broadcast_to(squares[None], (opt_count,) + squares.shape)
    squares = lax.all_to_all(squares, "opt", split_axis=0, concat_axis=0, tiled=True)
    totals = jnp.sum(squares[:, 0], axis=0)
    row_total, adam_total = totals[:row_blocks], totals[64 : 64 + row_blocks]
    graft_scale = jnp.sqrt(adam_total) / (jnp.sqrt(row_total) + EPS_GRAFT)
    master_new = master - LEARN_RATE * graft_scale[:, None, None] * rows

    low = after((grad - rounded).astype(jnp.bfloat16), squares)
    low_whole = lax.all_gather(low, "opt", axis=0)
    left_new, right_new = factors(block_at, used, high_whole, low_whole, factor_left, factor_right)
    weights = gather_weights(master_new.astype(jnp.bfloat16), parts.shape, place, left_new)
    return (master_new, moment_new, weights.reshape(-1, slab_rows, width), left_new, right_new)


def solution(mesh):
    placed = (
        P("dp", None, "opt", None),
        P("dp", "opt", None),
        P("dp", "opt", None),
        P(),
        P("dp", "opt", None, None, None),
        P("dp", "opt", None, None, None),
        P("dp", "opt", None, None, None),
        P("dp", "opt", None, None, None),
    )
    return jax.shard_map(
        shards,
        mesh=mesh,
        in_specs=placed,
        out_specs=(
            P("dp", "opt", None),
            P("dp", "opt", None),
            P(None, "opt", None),
            P("dp", "opt", None, None, None),
            P("dp", "opt", None, None, None),
        ),
        check_vma=False,
    )
```

```python
import functools

import jax
import jax.numpy as jnp
from jax import lax
from jax.experimental import pallas as pl
from jax.experimental.pallas import tpu as pltpu
from jax.sharding import PartitionSpec as P

BETA_FACTOR = 0.75
BETA_MOMENT = 0.95
LEARN_RATE = 0.1
EPS_ADAM = 1e-08
EPS_GRAFT = 1e-06
SIDE = 4
VMEM = 60 * 2**20


def shift_perm(axis, step):
    pairs = []
    for z in range(SIDE):
        for y in range(SIDE):
            to_z = (z + step) % SIDE if axis == "z" else z
            to_y = (y + step) % SIDE if axis == "y" else y
            pairs.append((z * SIDE + y, to_z * SIDE + to_y))
    return pairs


def send(value, axis, step):
    return lax.ppermute(value, "dp", shift_perm(axis, step))


def after(value, *earlier):
    return lax.optimization_barrier((value,) + earlier)[0]


ORDER = (("y", 1), ("z", 1), ("y", 3), ("z", 3), ("y", 2), ("z", 2))
OTHER = {"y": "z", "z": "y"}


def exchange(make):
    got = {}
    for axis, step in ORDER:
        value = make(axis, step)
        got[axis, step] = send(after(value, got["z", 1]) if (axis, step) == ORDER[-1] else value, axis, step)
    return got


def together(got):
    return dict(zip(got, lax.optimization_barrier(tuple(got.values()))))


def sum_replicas(parts, place, needed):
    blocks, half_rows, width = parts.shape[2], parts.shape[3] // 2, parts.shape[4]
    top = {"y": 0, "z": half_rows}

    def raw(axis, step):
        at = (place[axis] + step) % SIDE
        start = (0, at, 0, top[axis], 0) if axis == "y" else (at, 0, 0, top[axis], 0)
        size = (SIDE, 1) if axis == "y" else (1, SIDE)
        got = lax.dynamic_slice(parts, start, size + (blocks, half_rows, width))
        return got.reshape((SIDE, blocks, half_rows, width))

    near = together(exchange(raw))

    def total(axis, step):
        at = (place[axis] + step) % SIDE
        axis = OTHER[axis]
        start = (at, place["y"]) if axis == "y" else (place["z"], at)
        own = lax.dynamic_slice(parts, start + (0, top[axis], 0), (1, 1, blocks, half_rows, width))[0, 0]
        picked = [lax.dynamic_index_in_dim(near[axis, hop], at, 0, keepdims=False) for hop in (1, 3, 2)]
        own, one, three, two = [part.astype(jnp.float32) for part in [own] + picked]
        return (own + one) + (three + two)

    far = together(exchange(total))
    halves = []
    for axis in ("y", "z"):
        one, three, two = [far[OTHER[axis], step] for step in (1, 3, 2)]
        halves.append((total(OTHER[axis], 0) + one) + (after(three, *needed) + two))
    return jnp.concatenate(halves, axis=1)


def place_kernel(step, place_ref, *refs):
    out, sems = refs[-2:]
    pieces = refs[:-2]
    z, y = place_ref[0], place_ref[1]
    still_z, still_y = lax.rem(z + SIDE - step, SIDE), lax.rem(y + SIDE - step, SIDE)
    count = pieces[0].shape[0]
    rows = pieces[0].shape[2]
    copies = []
    for hop in range(SIDE):
        upper = out.at[still_z, lax.rem(y + SIDE - hop, SIDE), :, pl.ds(0, rows)]
        lower = out.at[lax.rem(z + SIDE - hop, SIDE), still_y, :, pl.ds(rows, rows)]
        for half, target in enumerate((upper, lower)):
            source = pieces[half * (SIDE // count) + hop // count].at[hop % count]
            copies.append(pltpu.make_async_copy(source, target, sems.at[half * SIDE + hop]))
    for copy in copies:
        copy.start()
    for copy in copies:
        copy.wait()


def put(out, shape, place, step, upper, lower):
    spot = jnp.stack([place["z"], place["y"]]).astype(jnp.int32)
    before = [] if out is None else [out]
    pieces = upper + lower
    piece = pl.BlockSpec(pieces[0].shape, lambda t: (0, 0, 0, 0))

    def kernel(place_ref, *refs):
        place_kernel(step, place_ref, *refs[: len(pieces)], *refs[-2:])

    return pl.pallas_call(
        kernel,
        grid=(1,),
        out_shape=jax.ShapeDtypeStruct(shape, jnp.bfloat16),
        in_specs=[pl.BlockSpec(memory_space=pltpu.SMEM)]
        + [piece] * len(pieces)
        + [pl.BlockSpec(memory_space=pl.ANY)] * len(before),
        out_specs=pl.BlockSpec(memory_space=pl.ANY),
        scratch_shapes=[pltpu.SemaphoreType.DMA((2 * SIDE,))],
        input_output_aliases={1 + len(pieces): 0} if before else {},
        compiler_params=pltpu.CompilerParams(vmem_limit_bytes=8 * 2**20),
        cost_estimate=pl.CostEstimate(
            flops=0, bytes_accessed=4 * sum(value.size for value in pieces), transcendentals=0
        ),
        name="place_weights",
    )(spot, *pieces, *before)


def direction_kernel(owner_ref, rank_ref, left_ref, grad_ref, right_ref, adam_ref, out_ref, square_ref):
    k = pl.program_id(0)
    width = right_ref.shape[-1]
    grad = grad_ref[...].reshape(width, width)
    half = jnp.dot(left_ref[0, 0], grad, preferred_element_type=jnp.float32).astype(jnp.bfloat16)
    rows = jnp.dot(half, right_ref[0, 0], preferred_element_type=jnp.float32)
    out_ref[0] = rows

    @pl.when(k == 0)
    def _():
        square_ref[...] = adam_ref[...]

    lane = lax.broadcasted_iota(jnp.int32, square_ref.shape, 1)
    square_ref[...] += jnp.where(lane == k, jnp.sum(rows * rows), 0.0)


def directions(owner, rank, left_rows, grad_whole, right_roots, adam_square):
    opt_count, blocks, slab_rows, width = grad_whole.shape
    grid_spec = pltpu.PrefetchScalarGridSpec(
        num_scalar_prefetch=2,
        grid=(blocks,),
        in_specs=[
            pl.BlockSpec((1, 1, slab_rows, width), lambda k, owner, rank: (rank[k], owner[k], 0, 0)),
            pl.BlockSpec((opt_count, 1, slab_rows, width), lambda k, owner, rank: (0, k, 0, 0)),
            pl.BlockSpec((1, 1, width, width), lambda k, owner, rank: (owner[k], rank[k], 0, 0)),
            pl.BlockSpec((8, 128), lambda k, owner, rank: (0, 0)),
        ],
        out_specs=[
            pl.BlockSpec((1, slab_rows, width), lambda k, owner, rank: (k, 0, 0)),
            pl.BlockSpec((8, 128), lambda k, owner, rank: (0, 0)),
        ],
    )
    flops = blocks * 4 * slab_rows * width * width
    return pl.pallas_call(
        direction_kernel,
        grid_spec=grid_spec,
        out_shape=[
            jax.ShapeDtypeStruct((blocks, slab_rows, width), jnp.float32),
            jax.ShapeDtypeStruct((8, 128), jnp.float32),
        ],
        compiler_params=pltpu.CompilerParams(vmem_limit_bytes=56 * 2**20),
        cost_estimate=pl.CostEstimate(
            flops=flops, bytes_accessed=blocks * width * width * 4, transcendentals=0
        ),
        name="directions",
    )(owner, rank, left_rows, grad_whole, right_roots, adam_square)


def gram_kernel(block_ref, used_ref, high_ref, low_ref, left_ref, right_ref, left_out, right_out):
    slot = pl.program_id(0)
    width = left_ref.shape[-1]

    @pl.when(used_ref[slot] == 1)
    def _():
        high = high_ref[...].reshape(width, width)
        low = low_ref[...].reshape(width, width)
        scale = (1.0 - BETA_FACTOR) / width

        def gram(dims):
            dot = functools.partial(
                lax.dot_general, dimension_numbers=(dims, ((), ())), preferred_element_type=jnp.float32
            )
            cross = dot(high, low)
            return dot(high, high) + (cross + cross.T)

        left_out[0, 0, 0] = BETA_FACTOR * left_ref[0, 0, 0] + scale * gram(((1,), (1,)))
        right_out[0, 0, 0] = BETA_FACTOR * right_ref[0, 0, 0] + scale * gram(((0,), (0,)))

    @pl.when(used_ref[slot] == 0)
    def _():
        left_out[...] = left_ref[...]
        right_out[...] = right_ref[...]


def factors(block_at, used, high, low, factor_left, factor_right):
    slot_count, width = factor_left.shape[2], factor_left.shape[-1]
    opt_count, _, slab_rows, _ = high.shape
    grad_spec = pl.BlockSpec((opt_count, 1, slab_rows, width), lambda s, at, used: (0, at[s], 0, 0))
    state_spec = pl.BlockSpec((1, 1, 1, width, width), lambda s, at, used: (0, 0, s, 0, 0))
    grid_spec = pltpu.PrefetchScalarGridSpec(
        num_scalar_prefetch=2,
        grid=(slot_count,),
        in_specs=[grad_spec, grad_spec, state_spec, state_spec],
        out_specs=[state_spec, state_spec],
    )
    return pl.pallas_call(
        gram_kernel,
        grid_spec=grid_spec,
        out_shape=[jax.ShapeDtypeStruct(factor_left.shape, jnp.float32)] * 2,
        compiler_params=pltpu.CompilerParams(vmem_limit_bytes=VMEM),
        cost_estimate=pl.CostEstimate(
            flops=slot_count * 12 * width**3,
            bytes_accessed=slot_count * 20 * width * width,
            transcendentals=0,
        ),
        name="factors",
    )(block_at, used, high, low, factor_left, factor_right)


def gather_weights(weights, shape, place, meanwhile):
    half_rows = weights.shape[1] // 2
    own = {"y": weights[:, :half_rows], "z": weights[:, half_rows:]}
    near = together(exchange(lambda axis, step: own[axis]))
    line = {axis: jnp.stack([own[axis]] + [near[axis, hop] for hop in (1, 2, 3)]) for axis in own}
    far = {(axis, step): send(line[OTHER[axis]], axis, step) for axis, step in ORDER[:4]}
    for axis in ("y", "z"):
        halves = [send(far[axis, 1][:2], axis, 1), send(far[axis, 3][2:], axis, 3)]
        far[axis, 2] = halves
    out = put(None, shape, place, 0, [line["y"]], [line["z"]])
    out = put(out, shape, place, 1, [far["z", 1]], [far["y", 1]])
    far["z", 3] = after(far["z", 3], meanwhile)
    out = put(out, shape, place, 3, [far["z", 3]], [far["y", 3]])
    return put(out, shape, place, 2, far["z", 2], far["y", 2])


def shards(
    grad_partial,
    master,
    second_moment,
    owner_table,
    factor_left,
    factor_right,
    root_left,
    root_right,
):
    opt_count = lax.axis_size("opt")
    slot_count = factor_left.shape[2]
    row_blocks, slab_rows, width = master.shape
    dp_at, opt_at = lax.axis_index("dp"), lax.axis_index("opt")
    place = {"z": dp_at // SIDE, "y": dp_at % SIDE}

    owner = lax.dynamic_slice_in_dim(owner_table[:, 0], dp_at * row_blocks, row_blocks, 0)
    position = jnp.arange(row_blocks)
    same_owner = owner[:, None] == owner[None, :]
    earlier = position[None, :] < position[:, None]
    rank = jnp.sum((same_owner & earlier).astype(jnp.int32), axis=1)
    mine = (owner[None, :] == opt_at) & (rank[None, :] == jnp.arange(slot_count)[:, None])
    used = jnp.sum(mine.astype(jnp.int32), axis=1)
    block_at = jnp.sum(jnp.where(mine, position[None, :], 0), axis=1).astype(jnp.int32)

    right_roots = lax.all_gather(root_right[0, 0], "opt", axis=0)
    left_rows = lax.all_to_all(
        root_left[0, 0].reshape(slot_count, opt_count, slab_rows, width),
        "opt",
        split_axis=1,
        concat_axis=1,
        tiled=True,
    )

    parts = grad_partial[0].reshape(SIDE, SIDE, row_blocks, slab_rows, width)
    grad = sum_replicas(parts, place, (left_rows, right_roots))

    rounded = lax.reduce_precision(grad, 8, 7)
    high = rounded.astype(jnp.bfloat16)
    high_whole = lax.all_gather(high, "opt", axis=0)
    moment_new = BETA_MOMENT * second_moment + (1.0 - BETA_MOMENT) * grad * grad
    step = grad / (jnp.sqrt(moment_new) + EPS_ADAM)
    adam_square = jnp.sum(step * step, axis=(1, 2))
    adam_tile = jnp.pad(adam_square[None], ((0, 7), (64, 64 - row_blocks)))
    rows, squares = directions(owner, rank, left_rows, high_whole, right_roots, adam_tile)
    squares = jnp.broadcast_to(squares[None], (opt_count,) + squares.shape)
    squares = lax.all_to_all(squares, "opt", split_axis=0, concat_axis=0, tiled=True)
    totals = jnp.sum(squares[:, 0], axis=0)
    row_total, adam_total = totals[:row_blocks], totals[64 : 64 + row_blocks]
    graft_scale = jnp.sqrt(adam_total) / (jnp.sqrt(row_total) + EPS_GRAFT)
    master_new = master - LEARN_RATE * graft_scale[:, None, None] * rows

    low = after((grad - rounded).astype(jnp.bfloat16), squares)
    low_whole = lax.all_gather(low, "opt", axis=0)
    left_new, right_new = factors(block_at, used, high_whole, low_whole, factor_left, factor_right)
    weights = gather_weights(master_new.astype(jnp.bfloat16), parts.shape, place, left_new)
    return (master_new, moment_new, weights.reshape(-1, slab_rows, width), left_new, right_new)


def solution(mesh):
    placed = (
        P("dp", None, "opt", None),
        P("dp", "opt", None),
        P("dp", "opt", None),
        P(),
        P("dp", "opt", None, None, None),
        P("dp", "opt", None, None, None),
        P("dp", "opt", None, None, None),
        P("dp", "opt", None, None, None),
    )
    return jax.shard_map(
        shards,
        mesh=mesh,
        in_specs=placed,
        out_specs=(
            P("dp", "opt", None),
            P("dp", "opt", None),
            P(None, "opt", None),
            P("dp", "opt", None, None, None),
            P("dp", "opt", None, None, None),
        ),
        check_vma=False,
    )
```
